32 devices in a mesh: groups: 2 (over y), cuts: 16 (over z, x, core).
Axes of the slice: x: 2, y: 2, z: 4, core: 2. Of those that a mesh axis runs over, the one named last changes fastest.
Arguments:
- estimate: float32 [4, 16, 128, 256], P('groups', 'cuts'), parts along dimension 0, may hold values from -6 to 6
- coil_maps: float32 [4, 16, 16, 128, 256], P('groups', None, 'cuts'), parts along dimension 0, may hold values from -3 to 3
- measured: float32 [4, 16, 16, 128, 256], P('groups', None, None, 'cuts'), parts along dimension 0, may hold values from -5 to 5
- sampled: int32 [32, 128], P('groups', 'cuts'), parts along dimension 0, may hold values 0 or 1
- plane_kernel: bfloat16 [3, 3, 2, 48], replicated, may hold values from -1.5 to 1.5
- depth_kernel: bfloat16 [3, 48, 48], replicated, may hold values from -0.5 to 0.5
- depth_offset: float32 [48], replicated, may hold values from -3 to 3
Outputs:
- next_image: float32 [4, 16, 128, 256], P('groups', 'cuts'), parts along dimension 0
The draws below stay inside these ranges and needn't reach their ends.
There are 2 independent parts, one for each index of `groups`. The reference program is written for one: setup_inputs(seed, part) draws one part's arguments, and reference() takes and returns one part's arrays. A program takes and returns all parts, laid end to end along the dimension named above; an argument that names none is the same for every part. Nothing has to cross between parts.
All inputs are finite; a program needn't handle non-finite values. No bound on the sum of `sampled` on one device may be relied on, other than what follows from the above.
Results may differ from the reference program's by a relative error of at most 0.0027.
Values may be sent and summed in bfloat16 or wider, within the bound.
A program may use at most 128 MiB of HBM per device.

```python
import jax
import jax.numpy as jnp
from jax import lax

NX = 256
NY = 128
COILS = 16
CH = 48
NZ = 16


def set_ends(array, rng, least, top_value):
    place = [jax.random.randint(jax.random.fold_in(rng, axis), (), 0, length) for axis, length in enumerate(array.shape)]
    longest = array.shape.index(max(array.shape))
    next_to = place[:longest] + [(place[longest] + 1) % array.shape[longest]] + place[longest + 1:]
    return array.at[tuple(place)].set(least).at[tuple(next_to)].set(top_value)


def level_of(key, extent, pieces, low, high):
    level = 1.0
    for position, shards_of in pieces:
        draws = jax.random.uniform(jax.random.fold_in(jax.random.fold_in(key, 6), position), (shards_of,), jnp.float32, low / len(pieces), high / len(pieces))
        level = level * jnp.repeat(jnp.exp(draws), extent[position] // shards_of).reshape((-1,) + (1,) * (len(extent) - 1 - position))
    return level


def normal_values(rng, shape, scale, reach, shards=(), kind=jnp.bfloat16):
    drawn = jax.random.normal(rng, shape, jnp.float32) * scale
    if len(shards) > 0:
        drawn = level_of(rng, shape, shards, -0.22, 0.18) * drawn
    return jnp.clip(drawn, min=-reach, max=reach).astype(kind)


def setup_inputs(seed: int = 0, part: int = 0) -> dict:
    splits = jax.random.split(jax.random.key(seed), 8)
    part_keys = jax.random.split(jax.random.fold_in(splits[7], part), 8)
    estimate = normal_values(part_keys[0], (2, NZ, NY, NX), 1.0, 6.0, ((1, 16),), jnp.float32)
    coil_maps = normal_values(part_keys[1], (2, COILS, NZ, NY, NX), 0.5, 3.0, ((2, 16),), jnp.float32)
    measured = normal_values(part_keys[2], (2, COILS, NZ, NY, NX), 0.7, 5.0, ((3, 16),), jnp.float32)
    sampled = set_ends((jax.random.randint(part_keys[3], (NZ, NY), 0, 3) < 1).astype(jnp.int32), jax.random.fold_in(part_keys[3], 1), 0, 1)
    plane_kernel = normal_values(splits[4], (3, 3, 2, CH), 18 ** -0.5, 1.5)
    depth_kernel = normal_values(splits[5], (3, CH, CH), (3 * CH) ** -0.5, 0.5)
    depth_offset = normal_values(splits[6], (CH,), 0.5, 3.0, (), jnp.float32)
    return {"estimate": estimate, "coil_maps": coil_maps, "measured": measured, "sampled": sampled, "plane_kernel": plane_kernel, "depth_kernel": depth_kernel, "depth_offset": depth_offset}


def plane_conv(volume, kernel):
    rows, columns = volume.shape[2], volume.shape[3]
    padded = jnp.pad(volume, ((0, 0), (0, 0), (1, 1), (1, 1)))
    summed = None
    for row_shift in range(3):
        for column_shift in range(3):
            piece = padded[:, :, row_shift:row_shift + rows, column_shift:column_shift + columns]
            term = jnp.einsum("ic,izyx->czyx", kernel[row_shift, column_shift], piece, precision=lax.Precision.HIGHEST)
            summed = term if summed is None else summed + term
    return summed


def plane_adjoint(volume, kernel):
    rows, columns = volume.shape[2], volume.shape[3]
    padded = jnp.pad(volume, ((0, 0), (0, 0), (1, 1), (1, 1)))
    summed = None
    for row_shift in range(3):
        for column_shift in range(3):
            piece = padded[:, :, 2 - row_shift:2 - row_shift + rows, 2 - column_shift:2 - column_shift + columns]
            term = jnp.einsum("ic,czyx->izyx", kernel[row_shift, column_shift], piece, precision=lax.Precision.HIGHEST)
            summed = term if summed is None else summed + term
    return summed


def reference(estimate, coil_maps, measured, sampled, plane_kernel, depth_kernel, depth_offset):
    ftype = estimate.dtype
    image_bf = estimate.astype(jnp.bfloat16)
    plane_wide = plane_kernel.astype(ftype)
    depth_wide = depth_kernel.astype(ftype)
    features = plane_conv(image_bf.astype(ftype), plane_wide).astype(jnp.bfloat16)
    padded_feat = jnp.pad(features.astype(ftype), ((0, 0), (1, 1), (0, 0), (0, 0)))
    preact = depth_offset[:, None, None, None]
    for tap_index in range(3):
        preact = preact + jnp.einsum("ic,izyx->czyx", depth_wide[tap_index], padded_feat[:, tap_index:tap_index + NZ], precision=lax.Precision.HIGHEST)
    activation = jnp.tanh(preact).astype(jnp.bfloat16)
    padded_act = jnp.pad(activation.astype(ftype), ((0, 0), (1, 1), (0, 0), (0, 0)))
    backward_mix = None
    for tap_index in range(3):
        term = jnp.einsum("ic,czyx->izyx", depth_wide[tap_index], padded_act[:, 2 - tap_index:2 - tap_index + NZ], precision=lax.Precision.HIGHEST)
        backward_mix = term if backward_mix is None else backward_mix + term
    regular = plane_adjoint(backward_mix, plane_wide)
    picture = estimate[0] + 1j * estimate[1]
    maps = coil_maps[0] + 1j * coil_maps[1]
    coil_images = maps * picture[None]
    kspace = jnp.fft.fftn(coil_images, axes=(1, 2, 3), norm="ortho")
    keep_mask = sampled.astype(ftype)[None, :, :, None]
    residual = keep_mask * (kspace - (measured[0] + 1j * measured[1]))
    errors = jnp.fft.ifftn(residual, axes=(1, 2, 3), norm="ortho")
    gradient = jnp.sum(jnp.conj(maps) * errors, axis=0)
    grad_parts = jnp.stack([jnp.real(gradient), jnp.imag(gradient)]).astype(ftype)
    return (estimate - 0.5 * grad_parts - 0.25 * regular).astype(jnp.float32)
```

```python
import math

import jax
import jax.numpy as jnp
import numpy as np
from jax import lax
from jax.sharding import PartitionSpec as P

step_size = 0.5
reg_weight = 0.25
bf16 = jnp.bfloat16
f32 = jnp.float32


def halves(table):
    high = jnp.asarray(table, f32).astype(bf16)
    low = (jnp.asarray(table, f32) - high.astype(f32)).astype(bf16)
    return high, low


def real_form(angles, factor):
    cos, sin = np.cos(angles) * factor, np.sin(angles) * factor
    return np.stack([np.stack([cos, sin]), np.stack([-sin, cos])])


def fourier(length):
    index = np.arange(length)
    angles = (index[:, None] * index[None, :] % length) * (2.0 * math.pi / length)
    return real_form(angles, 1.0 / math.sqrt(length))


def line_table(length, devices):
    blocks = fourier(length).transpose(0, 2, 1, 3)
    lines = length // devices
    blocks = blocks.reshape(2, devices, lines, 2 * length).transpose(1, 0, 2, 3)
    return blocks.reshape(2 * length, 2 * length).astype(np.float32)


def depth_table(depth, lines):
    table = fourier(depth)
    whole = np.einsum("pqkz,lm->pklzqm", table, np.eye(lines))
    return whole.reshape(2 * depth * lines, 2 * depth * lines).astype(np.float32)


def readout_table(length):
    table = fourier(length)
    return np.concatenate([table[0, 0], table[0, 1]], axis=1).astype(np.float32)


def product(pattern, a, b):
    return jnp.einsum(pattern, a, b, preferred_element_type=f32)


def product3(pattern, a, b):
    ah, al = halves(a)
    bh, bl = halves(b)
    return product(pattern, ah, bh) + product(pattern, al, bh) + product(pattern, ah, bl)


def with_halo(x, axis, dim):
    devices, length = lax.axis_size(axis), x.shape[dim]
    up = [(i, i + 1) for i in range(devices - 1)]
    down = [(j, i) for i, j in up]
    last = lax.slice_in_dim(x, length - 1, length, axis=dim)
    initial = lax.slice_in_dim(x, 0, 1, axis=dim)
    before = lax.ppermute(last, axis, up)
    after = lax.ppermute(initial, axis, down)
    return jnp.concatenate([before, x, after], axis=dim)


def regular_term(estimate, plane_kernel, depth_kernel, depth_offset):
    _, slices, rows, columns = estimate.shape
    channels = plane_kernel.shape[3]
    image = with_halo(estimate.astype(bf16), "cuts", 1)
    padded = jnp.pad(image, ((0, 0), (0, 0), (1, 1), (1, 1)))
    shifted = jnp.concatenate(
        [padded[:, :, a : a + rows, b : b + columns] for a in range(3) for b in range(3)], axis=0
    )
    flat = plane_kernel.reshape(18, channels)
    features = product("kc,kzyx->czyx", flat, shifted).astype(bf16)
    taps = jnp.concatenate([features[:, k : k + slices] for k in range(3)], axis=0)
    preact = depth_offset[:, None, None, None] + product(
        "kc,kzyx->czyx", depth_kernel.reshape(3 * channels, channels), taps
    )
    activation = jnp.tanh(preact).astype(bf16)
    joint = jnp.einsum(
        "abim,kmc->abkic",
        plane_kernel.astype(f32),
        depth_kernel.astype(f32),
        precision=lax.Precision.HIGHEST,
    )
    high, low = halves(joint.reshape(54, channels))
    both = jnp.concatenate([high, low], axis=1)
    spread = product("rc,czyx->rzyx", both, jnp.concatenate([activation, activation], axis=0))
    spread = spread.reshape(3, 3, 3, 2, slices, rows, columns)
    spread = jnp.pad(spread, [(0, 0)] * 5 + [(1, 1), (1, 1)])
    total = sum(
        spread[a, b, :, :, :, 2 - a : 2 - a + rows, 2 - b : 2 - b + columns]
        for a in range(3)
        for b in range(3)
    )
    devices = lax.axis_size("cuts")
    up = [(i, i + 1) for i in range(devices - 1)]
    below = lax.ppermute(total[2][:, slices - 1 :], "cuts", up)
    above = lax.ppermute(total[0][:, :1], "cuts", [(j, i) for i, j in up])
    regular = total[1] + jnp.concatenate([below, total[2][:, : slices - 1]], axis=1)
    return regular + jnp.concatenate([total[0][:, 1:], above], axis=1)


def shards(estimate, coil_maps, measured, sampled, plane_kernel, depth_kernel, depth_offset):
    devices = lax.axis_size("cuts")
    _, slices, rows, columns = estimate.shape
    coils = coil_maps.shape[1]
    depth, lines = sampled.shape
    table = line_table(rows, devices)
    maps_real, maps_imag = coil_maps[0], coil_maps[1]
    image_real, image_imag = estimate[0][None], estimate[1][None]
    coil = jnp.concatenate(
        [
            maps_real * image_real - maps_imag * image_imag,
            maps_real * image_imag + maps_imag * image_real,
        ],
        axis=2,
    )
    sent = product3("ky,czyx->kczx", table, coil).astype(bf16)
    sent = sent.reshape(devices, 2 * lines, coils, slices, columns).transpose(0, 3, 2, 1, 4)
    arrived = lax.all_to_all(sent, "cuts", split_axis=0, concat_axis=0, tiled=True)
    mix = depth_table(depth, lines)
    mask = jnp.broadcast_to(sampled.astype(f32)[None], (2, depth, lines)).reshape(-1, 1)
    masked = mix * mask
    gram = jnp.einsum("kr,kq->rq", mix, masked, precision=lax.Precision.HIGHEST)
    readout = product3(
        "kx,xn->kn", measured.reshape(2 * coils * depth * lines, columns), readout_table(columns)
    ).reshape(2, coils, depth, lines, 2, columns)
    cosines, sines = readout[:, :, :, :, 0], readout[:, :, :, :, 1]
    known = jnp.stack([cosines[0] - sines[1], cosines[1] + sines[0]])
    known = product3(
        "kr,kcx->rcx",
        masked,
        known.transpose(0, 2, 3, 1, 4).reshape(2 * depth * lines, coils, columns),
    )
    data = arrived.reshape(depth, coils, 2 * lines, columns).transpose(0, 2, 1, 3)
    data = data.reshape(2 * depth * lines, coils, columns)
    high, low = halves(gram)
    residual = product("rq,qcx->rcx", high, data) + product("rq,qcx->rcx", low, data) - known
    back = residual.astype(bf16).reshape(devices, slices, 2 * lines, coils, columns)
    back = lax.all_to_all(back, "cuts", split_axis=0, concat_axis=0, tiled=True)
    back = back.transpose(0, 2, 1, 3, 4).reshape(2 * rows, slices, coils, columns)
    high, low = halves(table)
    errors = product("ky,kzcx->yczx", high, back) + product("ky,kzcx->yczx", low, back)
    errors = errors.reshape(2, rows, coils, slices, columns).transpose(0, 2, 3, 1, 4)
    grad_real = jnp.sum(maps_real * errors[0] + maps_imag * errors[1], axis=0)
    grad_imag = jnp.sum(maps_real * errors[1] - maps_imag * errors[0], axis=0)
    gradient = jnp.stack([grad_real, grad_imag])
    regular = regular_term(estimate, plane_kernel, depth_kernel, depth_offset)
    return estimate - step_size * gradient - reg_weight * regular


def solution(mesh):
    return jax.shard_map(
        shards,
        mesh=mesh,
        in_specs=(
            P("groups", "cuts", None, None),
            P("groups", None, "cuts", None, None),
            P("groups", None, None, "cuts", None),
            P("groups", "cuts"),
            P(),
            P(),
            P(),
        ),
        out_specs=P("groups", "cuts", None, None),
        check_vma=False,
    )
```

```python
import functools
import math

import jax
import jax.numpy as jnp
import ml_dtypes
import numpy as np
from jax import lax
from jax.experimental import pallas as pl
from jax.experimental.pallas import tpu as pltpu
from jax.sharding import PartitionSpec as P

step_size = 0.5
reg_weight = 0.25
bf16 = jnp.bfloat16
f32 = jnp.float32


def halves(table):
    if isinstance(table, np.ndarray):
        high = table.astype(ml_dtypes.bfloat16)
        return high, (table - high.astype(np.float32)).astype(ml_dtypes.bfloat16)
    high = jnp.asarray(table, f32).astype(bf16)
    low = (jnp.asarray(table, f32) - high.astype(f32)).astype(bf16)
    return high, low


def real_form(angles, factor):
    cos, sin = np.cos(angles) * factor, np.sin(angles) * factor
    return np.stack([np.stack([cos, sin]), np.stack([-sin, cos])])


def fourier(length):
    index = np.arange(length)
    angles = (index[:, None] * index[None, :] % length) * (2.0 * math.pi / length)
    return real_form(angles, 1.0 / math.sqrt(length))


def line_table(length, devices):
    blocks = fourier(length).transpose(0, 2, 1, 3)
    lines = length // devices
    blocks = blocks.reshape(2, devices, lines, 2 * length).transpose(1, 0, 2, 3)
    return blocks.reshape(2 * length, 2 * length).astype(np.float32)


def depth_table(depth, lines):
    table = fourier(depth)
    whole = np.einsum("pqkz,lm->pklzqm", table, np.eye(lines))
    return whole.reshape(2 * depth * lines, 2 * depth * lines).astype(np.float32)


def readout_table(length):
    table = fourier(length)
    return np.concatenate([table[0, 0], table[0, 1]], axis=1).astype(np.float32)


def product(pattern, a, b):
    return jnp.einsum(pattern, a, b, preferred_element_type=f32)


def product3(pattern, a, b):
    ah, al = halves(a)
    bh, bl = halves(b)
    return product(pattern, ah, bh) + product(pattern, al, bh) + product(pattern, ah, bl)


def with_halo(x, axis, dim):
    devices, length = lax.axis_size(axis), x.shape[dim]
    up = [(i, i + 1) for i in range(devices - 1)]
    down = [(j, i) for i, j in up]
    last = lax.slice_in_dim(x, length - 1, length, axis=dim)
    initial = lax.slice_in_dim(x, 0, 1, axis=dim)
    before = lax.ppermute(last, axis, up)
    after = lax.ppermute(initial, axis, down)
    return jnp.concatenate([before, x, after], axis=dim)


def regular_term(estimate, plane_kernel, depth_kernel, depth_offset):
    _, slices, rows, columns = estimate.shape
    channels = plane_kernel.shape[3]
    image = with_halo(estimate.astype(bf16), "cuts", 1)
    padded = jnp.pad(image, ((0, 0), (0, 0), (1, 1), (1, 1)))
    shifted = jnp.concatenate(
        [padded[:, :, a : a + rows, b : b + columns] for a in range(3) for b in range(3)], axis=0
    )
    flat = plane_kernel.reshape(18, channels)
    features = product("kc,kzyx->czyx", flat, shifted).astype(bf16)
    taps = jnp.concatenate([features[:, k : k + slices] for k in range(3)], axis=0)
    preact = depth_offset[:, None, None, None] + product(
        "kc,kzyx->czyx", depth_kernel.reshape(3 * channels, channels), taps
    )
    activation = jnp.tanh(preact).astype(bf16)
    joint = jnp.einsum(
        "abim,kmc->abkic",
        plane_kernel.astype(f32),
        depth_kernel.astype(f32),
        precision=lax.Precision.HIGHEST,
    )
    high, low = halves(joint.reshape(54, channels))
    both = jnp.concatenate([high, low], axis=1)
    spread = product("rc,czyx->rzyx", both, jnp.concatenate([activation, activation], axis=0))
    spread = spread.reshape(3, 3, 3, 2, slices, rows, columns)
    spread = jnp.pad(spread, [(0, 0)] * 5 + [(1, 1), (1, 1)])
    total = sum(
        spread[a, b, :, :, :, 2 - a : 2 - a + rows, 2 - b : 2 - b + columns]
        for a in range(3)
        for b in range(3)
    )
    devices = lax.axis_size("cuts")
    up = [(i, i + 1) for i in range(devices - 1)]
    below = lax.ppermute(total[2][:, slices - 1 :], "cuts", up)
    above = lax.ppermute(total[0][:, :1], "cuts", [(j, i) for i, j in up])
    regular = total[1] + jnp.concatenate([below, total[2][:, : slices - 1]], axis=1)
    return regular + jnp.concatenate([total[0][:, 1:], above], axis=1)


def dot(a, b):
    return jnp.dot(a, b, preferred_element_type=f32)


def split(value):
    high = value.astype(bf16)
    return high, (value - high.astype(f32)).astype(bf16)


def dot3(ah, al, b):
    bh, bl = split(b)
    return dot(ah, bh) + dot(al, bh) + dot(ah, bl)


def kernel(
    chunks,
    estimate,
    maps_any,
    measured_any,
    mask,
    line_h,
    line_l,
    line_ht,
    line_lt,
    mix_ht,
    mix_lt,
    mix_h,
    mix_l,
    read_h,
    read_l,
    spread,
    spread_t,
    depth_rows,
    depth_t,
    offset,
    out,
    maps,
    measured,
    known,
    gram_h,
    gram_l,
    mixed_h,
    mixed_l,
    send1,
    recv1,
    send2,
    recv2,
    image,
    halo,
    patches,
    total,
    edges,
    edges_in,
    centre,
    map_sem,
    measured_sem,
    send1_sem,
    recv1_sem,
    send2_sem,
    recv2_sem,
    halo_send,
    halo_recv,
    edge_send,
    edge_recv,
):
    devices = send1.shape[1]
    me = lax.axis_index("cuts")
    above, below = lax.rem(me + 1, devices), lax.rem(me + devices - 1, devices)
    _, rows, columns = estimate.shape
    coils = maps.shape[1]
    group = coils // chunks
    block = send1.shape[2] // group

    def map_copy(q):
        part = pl.ds(q * group, group)
        return pltpu.make_async_copy(maps_any.at[:, part], maps.at[:, part], map_sem.at[q])

    measured_copy = pltpu.make_async_copy(measured_any, measured, measured_sem)
    for q in range(chunks):
        map_copy(q).start()
    measured_copy.start()

    barrier = pltpu.get_barrier_semaphore()

    def greet(step, carry):
        pl.semaphore_signal(
            barrier,
            inc=1,
            device_id={"cuts": lax.rem(me + step, devices)},
            device_id_type=pl.DeviceIdType.MESH,
        )
        return carry

    lax.fori_loop(1, devices, greet, 0)
    image[...] = estimate[...].astype(bf16)

    def remote(source, target, send_sem, recv_sem, device):
        return pltpu.make_async_remote_copy(
            src_ref=source,
            dst_ref=target,
            send_sem=send_sem,
            recv_sem=recv_sem,
            device_id={"cuts": device},
            device_id_type=pl.DeviceIdType.MESH,
        )

    halo_copies = [
        remote(image, halo.at[0], halo_send.at[0], halo_recv.at[0], above),
        remote(image, halo.at[1], halo_send.at[1], halo_recv.at[1], below),
    ]
    edge_copies = [
        remote(edges.at[0], edges_in.at[0], edge_send.at[0], edge_recv.at[0], above),
        remote(edges.at[1], edges_in.at[1], edge_send.at[1], edge_recv.at[1], below),
    ]

    def send_all(source, target, send_sem, recv_sem, q):
        def body(step, carry):
            device = lax.rem(me + step, devices)
            remote(
                source.at[q, device],
                target.at[q, me],
                send_sem.at[q, device],
                recv_sem.at[q, me],
                device,
            ).start()
            return carry

        lax.fori_loop(1, devices, body, 0)

    def wait_all(source, target, send_sem, recv_sem, q, sent):
        def body(step, carry):
            device = lax.rem(me + step, devices)
            copy = remote(
                source.at[q, device],
                target.at[q, device],
                send_sem.at[q, device],
                recv_sem.at[q, device],
                device,
            )
            if sent:
                copy.wait_send()
            else:
                copy.wait_recv()
            return carry

        lax.fori_loop(1, devices, body, 0)

    def lanes(pieces):
        return jnp.concatenate(pieces, axis=1)

    def put(target, mine, q, value):
        value = value.astype(bf16)
        for c in range(group):
            piece = value[:, c * columns : (c + 1) * columns]
            target[q, :, c * block : (c + 1) * block, :] = piece.reshape(devices, block, columns)
        mine[q, me] = target[q, me]

    def take(source, q):
        return lanes(
            [
                source[q, :, c * block : (c + 1) * block, :].reshape(devices * block, columns)
                for c in range(group)
            ]
        )

    def first(q):
        map_copy(q).wait()
        pieces = []
        for c in range(group):
            real, imag = maps[0, q * group + c], maps[1, q * group + c]
            pieces.append(
                jnp.concatenate(
                    [
                        real * estimate[0] - imag * estimate[1],
                        real * estimate[1] + imag * estimate[0],
                    ],
                    axis=0,
                )
            )
        put(send1, recv1, q, dot3(line_h[...], line_l[...], lanes(pieces)))

    first(0)
    pl.semaphore_wait(barrier, devices - 1)
    send_all(send1, recv1, send1_sem, recv1_sem, 0)
    for copy in halo_copies:
        copy.start()

    def first_rest(q, carry):
        first(q)
        send_all(send1, recv1, send1_sem, recv1_sem, q)
        return carry

    lax.fori_loop(1, chunks, first_rest, 0)

    for copy in halo_copies:
        copy.wait()
    has_below = jnp.where(me > 0, 1.0, 0.0).astype(f32)
    has_above = jnp.where(me < devices - 1, 1.0, 0.0).astype(f32)
    patches[0] = jnp.zeros(patches.shape[1:], bf16)
    patches[rows + 1] = jnp.zeros(patches.shape[1:], bf16)
    total[...] = jnp.zeros_like(total)
    step16 = 16

    def shift(value, way):
        axis = value.ndim - 1
        lane = lax.broadcasted_iota(jnp.int32, value.shape, axis)
        if way > 0:
            return jnp.where(lane == 0, 0.0, pltpu.roll(value, 1, axis))
        return jnp.where(lane == columns - 1, 0.0, pltpu.roll(value, columns - 1, axis))

    def build(t, carry):
        y = pl.multiple_of(t * step16, step16)
        stacked = jnp.concatenate(
            [
                halo[0, :, pl.ds(y, step16)].astype(f32) * has_below,
                image[:, pl.ds(y, step16)].astype(f32),
                halo[1, :, pl.ds(y, step16)].astype(f32) * has_above,
                jnp.zeros((2, step16, columns), f32),
            ],
            axis=0,
        )
        turned = jnp.swapaxes(stacked, 0, 1)
        left = shift(turned.reshape(step16 * 8, columns), 1).reshape(turned.shape)
        right = shift(turned.reshape(step16 * 8, columns), -1).reshape(turned.shape)
        patches[pl.ds(y + 1, step16)] = jnp.concatenate(
            [left, turned, right, jnp.zeros_like(turned)], axis=1
        ).astype(bf16)
        return carry

    lax.fori_loop(0, rows // step16, build, 0)
    joint_h, joint_l = split(dot(spread[...], depth_rows[...]))
    size = 8

    def regularize(t, carry):
        y = t * size
        patch = lanes(
            [
                jnp.concatenate([patches[y + j + a] for a in range(3)], axis=0)
                for j in range(size)
            ]
        )
        features = dot(spread_t[...], patch).astype(bf16)
        activation = jnp.tanh(dot(depth_t[...], features) + offset[...]).astype(bf16)
        back = dot(joint_h, activation) + dot(joint_l, activation)
        for j in range(size):
            piece = back[:, j * columns : (j + 1) * columns]
            for a in range(3):
                top = a * 32
                total[y + j + a] += (
                    shift(piece[top : top + 8], -1)
                    + piece[top + 8 : top + 16]
                    + shift(piece[top + 16 : top + 24], 1)
                )
        return carry

    lax.fori_loop(0, rows // size, regularize, 0)

    def unload(t, carry):
        y = pl.multiple_of(t * step16, step16)
        turned = jnp.swapaxes(total[pl.ds(y + 1, step16)], 0, 1)
        edges[1, :, pl.ds(y, step16)] = turned[0:2].astype(bf16)
        centre[:, pl.ds(y, step16)] = turned[2:4]
        edges[0, :, pl.ds(y, step16)] = turned[4:6].astype(bf16)
        return carry

    lax.fori_loop(0, rows // step16, unload, 0)
    for copy in edge_copies:
        copy.start()

    masked_h = mix_ht[...].astype(f32) * mask[...]
    masked_l = mix_lt[...].astype(f32) * mask[...]
    mixed_h[...] = masked_h.astype(bf16)
    mixed_l[...] = masked_l.astype(bf16)
    high, low = split(
        dot(mixed_h[...], mix_h[...]) + dot(mixed_l[...], mix_h[...]) + dot(mixed_h[...], mix_l[...])
    )
    gram_h[...] = high
    gram_l[...] = low
    measured_copy.wait()

    def acquire(c, carry):
        value = measured[:, c].reshape(devices * block, columns)
        value_h, value_l = split(value)
        wide = dot(value_h, read_h[...]) + dot(value_l, read_h[...]) + dot(value_h, read_l[...])
        half = devices * block // 2
        cos, sin = wide[:, :columns], wide[:, columns:]
        turned = jnp.concatenate([cos[:half] - sin[half:], cos[half:] + sin[:half]], axis=0)
        known[c] = dot3(mixed_h[...], mixed_l[...], turned)
        return carry

    lax.fori_loop(0, coils, acquire, 0)

    def second(q, carry):
        wait_all(send1, recv1, send1_sem, recv1_sem, q, False)
        data = take(recv1, q)
        value = dot(gram_h[...], data) + dot(gram_l[...], data)
        put(send2, recv2, q, value - lanes([known[q * group + c] for c in range(group)]))
        send_all(send2, recv2, send2_sem, recv2_sem, q)
        return carry

    lax.fori_loop(0, chunks, second, 0)

    for copy in edge_copies:
        copy.wait()
    regular = (
        centre[...]
        + edges_in[0].astype(f32) * has_below
        + edges_in[1].astype(f32) * has_above
    )
    out[...] = estimate[...] - reg_weight * regular

    def third(q, carry):
        wait_all(send2, recv2, send2_sem, recv2_sem, q, False)
        data = take(recv2, q)
        errors = dot(line_ht[...], data) + dot(line_lt[...], data)
        real, imag = 0.0, 0.0
        for c in range(group):
            error = errors[:, c * columns : (c + 1) * columns]
            map_real, map_imag = maps[0, q * group + c], maps[1, q * group + c]
            real += map_real * error[:rows] + map_imag * error[rows:]
            imag += map_real * error[rows:] - map_imag * error[:rows]
        out[0] -= step_size * real
        out[1] -= step_size * imag
        return carry

    lax.fori_loop(0, chunks, third, 0)

    def drain(q, carry):
        wait_all(send1, recv1, send1_sem, recv1_sem, q, True)
        wait_all(send2, recv2, send2_sem, recv2_sem, q, True)
        return carry

    lax.fori_loop(0, chunks, drain, 0)


def fused(estimate, coil_maps, measured, sampled, plane_kernel, depth_kernel, depth_offset):
    devices = lax.axis_size("cuts")
    _, _, rows, columns = estimate.shape
    coils = coil_maps.shape[1]
    depth, lines = sampled.shape
    channels = plane_kernel.shape[3]
    chunks = 4
    table = line_table(rows, devices)
    mix = depth_table(depth, lines)
    mask = jnp.broadcast_to(sampled.astype(f32)[None], (2, depth, lines)).reshape(1, -1)
    wide = jnp.pad(plane_kernel, ((0, 0), (0, 1), (0, 0), (0, 0)))
    taps = np.eye(4, 3, dtype=np.float32)
    spread = (
        wide[:, :, None, :, None, :] * jnp.asarray(taps, bf16)[None, None, :, None, :, None]
    ).reshape(96, 3 * channels)
    depth_rows = depth_kernel.reshape(3 * channels, channels)
    rest = [
        mask,
        *halves(table),
        *halves(table.T),
        *halves(mix.T),
        *halves(mix),
        *halves(readout_table(columns)),
        spread,
        spread.T,
        depth_rows,
        depth_rows.T,
        depth_offset[:, None],
    ]
    size = 2 * rows
    packet = (chunks, devices, coils // chunks * 2 * lines, columns)
    vmem = pltpu.VMEM
    pair = pltpu.SemaphoreType.DMA((chunks, devices))
    two = pltpu.SemaphoreType.DMA((2,))
    square = vmem((size, size), bf16)
    result = pl.pallas_call(
        functools.partial(kernel, chunks),
        out_shape=jax.ShapeDtypeStruct((2, rows, columns), f32),
        in_specs=[pl.BlockSpec(memory_space=vmem)]
        + [pl.BlockSpec(memory_space=pl.ANY)] * 2
        + [pl.BlockSpec(memory_space=vmem)] * len(rest),
        out_specs=pl.BlockSpec(memory_space=vmem),
        scratch_shapes=[
            vmem((2, coils, rows, columns), f32),
            vmem(measured.shape, f32),
            vmem((coils, size, columns), f32),
            square,
            square,
            square,
            square,
            vmem(packet, bf16),
            vmem(packet, bf16),
            vmem(packet, bf16),
            vmem(packet, bf16),
            vmem((2, rows, columns), bf16),
            vmem((2, 2, rows, columns), bf16),
            vmem((rows + 2, 32, columns), bf16),
            vmem((rows + 2, 8, columns), f32),
            vmem((2, 2, rows, columns), bf16),
            vmem((2, 2, rows, columns), bf16),
            vmem((2, rows, columns), f32),
            pltpu.SemaphoreType.DMA((chunks,)),
            pltpu.SemaphoreType.DMA,
            pair,
            pair,
            pair,
            pair,
            two,
            two,
            two,
            two,
        ],
        compiler_params=pltpu.CompilerParams(
            collective_id=0, has_side_effects=True, vmem_limit_bytes=52 * 2**20
        ),
    )(estimate[:, 0], coil_maps[:, :, 0], measured, *rest)
    return result[:, None]


def shards(estimate, coil_maps, measured, sampled, plane_kernel, depth_kernel, depth_offset):
    devices = lax.axis_size("cuts")
    _, slices, rows, columns = estimate.shape
    coils = coil_maps.shape[1]
    depth, lines = sampled.shape
    if slices == 1 and 2 * lines % 16 == 0 and rows % 16 == 0 and coils % 4 == 0:
        return fused(
            estimate, coil_maps, measured, sampled, plane_kernel, depth_kernel, depth_offset
        )
    table = line_table(rows, devices)
    maps_real, maps_imag = coil_maps[0], coil_maps[1]
    image_real, image_imag = estimate[0][None], estimate[1][None]
    coil = jnp.concatenate(
        [
            maps_real * image_real - maps_imag * image_imag,
            maps_real * image_imag + maps_imag * image_real,
        ],
        axis=2,
    )
    sent = product3("ky,czyx->kczx", table, coil).astype(bf16)
    sent = sent.reshape(devices, 2 * lines, coils, slices, columns).transpose(0, 3, 2, 1, 4)
    arrived = lax.all_to_all(sent, "cuts", split_axis=0, concat_axis=0, tiled=True)
    mix = depth_table(depth, lines)
    mask = jnp.broadcast_to(sampled.astype(f32)[None], (2, depth, lines)).reshape(-1, 1)
    masked = mix * mask
    gram = jnp.einsum("kr,kq->rq", mix, masked, precision=lax.Precision.HIGHEST)
    readout = product3(
        "kx,xn->kn", measured.reshape(2 * coils * depth * lines, columns), readout_table(columns)
    ).reshape(2, coils, depth, lines, 2, columns)
    cosines, sines = readout[:, :, :, :, 0], readout[:, :, :, :, 1]
    known = jnp.stack([cosines[0] - sines[1], cosines[1] + sines[0]])
    known = product3(
        "kr,kcx->rcx",
        masked,
        known.transpose(0, 2, 3, 1, 4).reshape(2 * depth * lines, coils, columns),
    )
    data = arrived.reshape(depth, coils, 2 * lines, columns).transpose(0, 2, 1, 3)
    data = data.reshape(2 * depth * lines, coils, columns)
    high, low = halves(gram)
    residual = product("rq,qcx->rcx", high, data) + product("rq,qcx->rcx", low, data) - known
    back = residual.astype(bf16).reshape(devices, slices, 2 * lines, coils, columns)
    back = lax.all_to_all(back, "cuts", split_axis=0, concat_axis=0, tiled=True)
    back = back.transpose(0, 2, 1, 3, 4).reshape(2 * rows, slices, coils, columns)
    high, low = halves(table)
    errors = product("ky,kzcx->yczx", high, back) + product("ky,kzcx->yczx", low, back)
    errors = errors.reshape(2, rows, coils, slices, columns).transpose(0, 2, 3, 1, 4)
    grad_real = jnp.sum(maps_real * errors[0] + maps_imag * errors[1], axis=0)
    grad_imag = jnp.sum(maps_real * errors[1] - maps_imag * errors[0], axis=0)
    gradient = jnp.stack([grad_real, grad_imag])
    regular = regular_term(estimate, plane_kernel, depth_kernel, depth_offset)
    return estimate - step_size * gradient - reg_weight * regular


def solution(mesh):
    return jax.shard_map(
        shards,
        mesh=mesh,
        in_specs=(
            P("groups", "cuts", None, None),
            P("groups", None, "cuts", None, None),
            P("groups", None, None, "cuts", None),
            P("groups", "cuts"),
            P(),
            P(),
            P(),
        ),
        out_specs=P("groups", "cuts", None, None),
        check_vma=False,
    )
```

```python
import functools
import math

import jax
import jax.numpy as jnp
import ml_dtypes
import numpy as np
from jax import lax
from jax.experimental import pallas as pl
from jax.experimental.pallas import tpu as pltpu
from jax.sharding import PartitionSpec as P

step_size = 0.5
reg_weight = 0.25
bf16 = jnp.bfloat16
f32 = jnp.float32


def halves(table):
    if isinstance(table, np.ndarray):
        high = table.astype(ml_dtypes.bfloat16)
        return high, (table - high.astype(np.float32)).astype(ml_dtypes.bfloat16)
    high = jnp.asarray(table, f32).astype(bf16)
    low = (jnp.asarray(table, f32) - high.astype(f32)).astype(bf16)
    return high, low


def real_form(angles, factor):
    cos, sin = np.cos(angles) * factor, np.sin(angles) * factor
    return np.stack([np.stack([cos, sin]), np.stack([-sin, cos])])


def fourier(length):
    index = np.arange(length)
    angles = (index[:, None] * index[None, :] % length) * (2.0 * math.pi / length)
    return real_form(angles, 1.0 / math.sqrt(length))


def line_table(length, devices):
    blocks = fourier(length).transpose(0, 2, 1, 3)
    lines = length // devices
    blocks = blocks.reshape(2, devices, lines, 2 * length).transpose(1, 0, 2, 3)
    return blocks.reshape(2 * length, 2 * length).astype(np.float32)


def depth_table(depth, lines):
    table = fourier(depth)
    whole = np.einsum("pqkz,lm->pklzqm", table, np.eye(lines))
    return whole.reshape(2 * depth * lines, 2 * depth * lines).astype(np.float32)


def readout_table(length):
    table = fourier(length)
    return np.concatenate([table[0, 0], table[0, 1]], axis=1).astype(np.float32)


def product(pattern, a, b):
    return jnp.einsum(pattern, a, b, preferred_element_type=f32)


def product3(pattern, a, b):
    ah, al = halves(a)
    bh, bl = halves(b)
    return product(pattern, ah, bh) + product(pattern, al, bh) + product(pattern, ah, bl)


def with_halo(x, axis, dim):
    devices, length = lax.axis_size(axis), x.shape[dim]
    up = [(i, i + 1) for i in range(devices - 1)]
    down = [(j, i) for i, j in up]
    last = lax.slice_in_dim(x, length - 1, length, axis=dim)
    initial = lax.slice_in_dim(x, 0, 1, axis=dim)
    before = lax.ppermute(last, axis, up)
    after = lax.ppermute(initial, axis, down)
    return jnp.concatenate([before, x, after], axis=dim)


def regular_term(estimate, plane_kernel, depth_kernel, depth_offset):
    _, slices, rows, columns = estimate.shape
    channels = plane_kernel.shape[3]
    image = with_halo(estimate.astype(bf16), "cuts", 1)
    padded = jnp.pad(image, ((0, 0), (0, 0), (1, 1), (1, 1)))
    shifted = jnp.concatenate(
        [padded[:, :, a : a + rows, b : b + columns] for a in range(3) for b in range(3)], axis=0
    )
    flat = plane_kernel.reshape(18, channels)
    features = product("kc,kzyx->czyx", flat, shifted).astype(bf16)
    taps = jnp.concatenate([features[:, k : k + slices] for k in range(3)], axis=0)
    preact = depth_offset[:, None, None, None] + product(
        "kc,kzyx->czyx", depth_kernel.reshape(3 * channels, channels), taps
    )
    activation = jnp.tanh(preact).astype(bf16)
    joint = jnp.einsum(
        "abim,kmc->abkic",
        plane_kernel.astype(f32),
        depth_kernel.astype(f32),
        precision=lax.Precision.HIGHEST,
    )
    high, low = halves(joint.reshape(54, channels))
    both = jnp.concatenate([high, low], axis=1)
    spread = product("rc,czyx->rzyx", both, jnp.concatenate([activation, activation], axis=0))
    spread = spread.reshape(3, 3, 3, 2, slices, rows, columns)
    spread = jnp.pad(spread, [(0, 0)] * 5 + [(1, 1), (1, 1)])
    total = sum(
        spread[a, b, :, :, :, 2 - a : 2 - a + rows, 2 - b : 2 - b + columns]
        for a in range(3)
        for b in range(3)
    )
    devices = lax.axis_size("cuts")
    up = [(i, i + 1) for i in range(devices - 1)]
    below = lax.ppermute(total[2][:, slices - 1 :], "cuts", up)
    above = lax.ppermute(total[0][:, :1], "cuts", [(j, i) for i, j in up])
    regular = total[1] + jnp.concatenate([below, total[2][:, : slices - 1]], axis=1)
    return regular + jnp.concatenate([total[0][:, 1:], above], axis=1)


def dot(a, b):
    return jnp.dot(a, b, preferred_element_type=f32)


def split(value):
    high = value.astype(bf16)
    return high, (value - high.astype(f32)).astype(bf16)


def dot3(ah, al, b):
    bh, bl = split(b)
    return dot(ah, bh) + dot(al, bh) + dot(ah, bl)


def kernel(
    chunks,
    estimate_any,
    maps_any,
    measured_any,
    tables_any,
    mask,
    spread,
    spread_t,
    depth_rows,
    offset,
    out,
    estimate,
    tables,
    maps,
    measured,
    known,
    gram_h,
    gram_l,
    mixed_h,
    mixed_l,
    send1,
    recv1,
    send2,
    recv2,
    image,
    halo,
    patches,
    total,
    edges,
    edges_in,
    centre,
    map_sem,
    measured_sem,
    estimate_sem,
    line_sem,
    table_sem,
    send1_sem,
    recv1_sem,
    send2_sem,
    recv2_sem,
    halo_send,
    halo_recv,
    edge_send,
    edge_recv,
):
    devices = send1.shape[1]
    me = lax.axis_index("cuts")
    above, below = lax.rem(me + 1, devices), lax.rem(me + devices - 1, devices)
    _, rows, columns = estimate.shape
    coils = maps.shape[1]
    bits = devices.bit_length() - 1

    def partner(step):
        if devices != 2**bits:
            return lax.rem(me + step, devices)
        device = 0
        for bit in range(bits):
            flip = (step // 2 ** (bits - 1 - bit)) % 2
            device += 2**bit * ((me // 2**bit + flip) % 2)
        return device

    group = coils // chunks
    block = send1.shape[2] // group

    def map_copy(q):
        part = pl.ds(q * group, group)
        return pltpu.make_async_copy(maps_any.at[:, part], maps.at[:, part], map_sem.at[q])

    def table_copy(first, count, sem):
        part = pl.ds(first, count)
        return pltpu.make_async_copy(tables_any.at[part], tables.at[part], sem)

    measured_copy = pltpu.make_async_copy(measured_any, measured, measured_sem)
    estimate_copy = pltpu.make_async_copy(estimate_any, estimate, estimate_sem)
    line_copy = table_copy(0, 2, line_sem)
    rest_copy = table_copy(2, tables.shape[0] - 2, table_sem)
    line_h, line_l, line_ht, line_lt = (tables.at[i] for i in range(4))
    mix_ht, mix_lt, mix_h, mix_l = (tables.at[i] for i in range(4, 8))
    estimate_copy.start()
    line_copy.start()
    for q in range(chunks):
        map_copy(q).start()
    rest_copy.start()
    measured_copy.start()

    barrier = pltpu.get_barrier_semaphore()

    def greet(step, carry):
        pl.semaphore_signal(
            barrier,
            inc=1,
            device_id={"cuts": lax.rem(me + step, devices)},
            device_id_type=pl.DeviceIdType.MESH,
        )
        return carry

    lax.fori_loop(1, devices, greet, 0)
    estimate_copy.wait()
    image[...] = estimate[...].astype(bf16)
    line_copy.wait()

    def remote(source, target, send_sem, recv_sem, device):
        return pltpu.make_async_remote_copy(
            src_ref=source,
            dst_ref=target,
            send_sem=send_sem,
            recv_sem=recv_sem,
            device_id={"cuts": device},
            device_id_type=pl.DeviceIdType.MESH,
        )

    halo_copies = [
        remote(image, halo.at[0], halo_send.at[0], halo_recv.at[0], above),
        remote(image, halo.at[1], halo_send.at[1], halo_recv.at[1], below),
    ]
    edge_copies = [
        remote(edges.at[0], edges_in.at[0], edge_send.at[0], edge_recv.at[0], above),
        remote(edges.at[1], edges_in.at[1], edge_send.at[1], edge_recv.at[1], below),
    ]

    def send_all(source, target, send_sem, recv_sem, q):
        def body(step, carry):
            device = partner(step)
            remote(
                source.at[q, device],
                target.at[q, me],
                send_sem.at[q, device],
                recv_sem.at[q, me],
                device,
            ).start()
            return carry

        lax.fori_loop(1, devices, body, 0)

    def wait_all(source, target, send_sem, recv_sem, q, sent):
        def body(step, carry):
            device = lax.rem(me + step, devices)
            copy = remote(
                source.at[q, device],
                target.at[q, device],
                send_sem.at[q, device],
                recv_sem.at[q, device],
                device,
            )
            if sent:
                copy.wait_send()
            else:
                copy.wait_recv()
            return carry

        lax.fori_loop(1, devices, body, 0)

    def lanes(pieces):
        return jnp.concatenate(pieces, axis=1)

    def put(target, mine, q, value):
        value = value.astype(bf16)
        for c in range(group):
            piece = value[:, c * columns : (c + 1) * columns]
            target[q, :, c * block : (c + 1) * block, :] = piece.reshape(devices, block, columns)
        mine[q, me] = target[q, me]

    def take(source, q):
        return lanes(
            [
                source[q, :, c * block : (c + 1) * block, :].reshape(devices * block, columns)
                for c in range(group)
            ]
        )

    def first(q):
        map_copy(q).wait()
        pieces = []
        for c in range(group):
            real, imag = maps[0, q * group + c], maps[1, q * group + c]
            pieces.append(
                jnp.concatenate(
                    [
                        real * estimate[0] - imag * estimate[1],
                        real * estimate[1] + imag * estimate[0],
                    ],
                    axis=0,
                )
            )
        put(send1, recv1, q, dot3(line_h[...], line_l[...], lanes(pieces)))

    first(0)
    pl.semaphore_wait(barrier, devices - 1)
    send_all(send1, recv1, send1_sem, recv1_sem, 0)
    for copy in halo_copies:
        copy.start()

    def first_rest(q, carry):
        first(q)
        send_all(send1, recv1, send1_sem, recv1_sem, q)
        return carry

    lax.fori_loop(1, chunks, first_rest, 0)

    rest_copy.wait()
    masked_h = mix_ht[...].astype(f32) * mask[...]
    masked_l = mix_lt[...].astype(f32) * mask[...]
    mixed_h[...] = masked_h.astype(bf16)
    mixed_l[...] = masked_l.astype(bf16)
    high, low = split(
        dot(mixed_h[...], mix_h[...]) + dot(mixed_l[...], mix_h[...]) + dot(mixed_h[...], mix_l[...])
    )
    gram_h[...] = high
    gram_l[...] = low
    measured_copy.wait()

    def acquire(c, carry):
        value = measured[:, c].reshape(devices * block, columns)
        value_h, value_l = split(value)
        cos = dot(value_h, tables[8]) + dot(value_l, tables[8]) + dot(value_h, tables[9])
        sin = dot(value_h, tables[10]) + dot(value_l, tables[10]) + dot(value_h, tables[11])
        half = devices * block // 2
        turned = jnp.concatenate([cos[:half] - sin[half:], cos[half:] + sin[:half]], axis=0)
        known[c] = dot3(mixed_h[...], mixed_l[...], turned)
        return carry

    lax.fori_loop(0, coils, acquire, 0)

    for copy in halo_copies:
        copy.wait()
    has_below = jnp.where(me > 0, 1.0, 0.0).astype(f32)
    has_above = jnp.where(me < devices - 1, 1.0, 0.0).astype(f32)
    patches[0] = jnp.zeros(patches.shape[1:], bf16)
    patches[rows + 1] = jnp.zeros(patches.shape[1:], bf16)
    total[...] = jnp.zeros_like(total)
    step16 = 16

    def shift(value, way):
        axis = value.ndim - 1
        lane = lax.broadcasted_iota(jnp.int32, value.shape, axis)
        if way > 0:
            return jnp.where(lane == 0, 0.0, pltpu.roll(value, 1, axis))
        return jnp.where(lane == columns - 1, 0.0, pltpu.roll(value, columns - 1, axis))

    def build(t, carry):
        y = pl.multiple_of(t * step16, step16)
        stacked = jnp.concatenate(
            [
                halo[0, :, pl.ds(y, step16)].astype(f32) * has_below,
                image[:, pl.ds(y, step16)].astype(f32),
                halo[1, :, pl.ds(y, step16)].astype(f32) * has_above,
                jnp.zeros((2, step16, columns), f32),
            ],
            axis=0,
        )
        turned = jnp.swapaxes(stacked, 0, 1)
        left = shift(turned.reshape(step16 * 8, columns), 1).reshape(turned.shape)
        right = shift(turned.reshape(step16 * 8, columns), -1).reshape(turned.shape)
        patches[pl.ds(y + 1, step16)] = jnp.concatenate(
            [left, turned, right, jnp.zeros_like(turned)], axis=1
        ).astype(bf16)
        return carry

    lax.fori_loop(0, rows // step16, build, 0)
    joint_h, joint_l = split(dot(spread[...], depth_rows[...]))
    size = 8

    def regularize(t, carry):
        y = t * size
        patch = lanes(
            [
                jnp.concatenate([patches[y + j + a] for a in range(3)], axis=0)
                for j in range(size)
            ]
        )
        features = dot(spread_t[...], patch).astype(bf16)
        activation = jnp.tanh(lax.dot_general(depth_rows[...], features, (((0,), (0,)), ((), ())), preferred_element_type=f32) + offset[...]).astype(bf16)
        back = dot(joint_h, activation) + dot(joint_l, activation)
        for j in range(size):
            piece = back[:, j * columns : (j + 1) * columns]
            for a in range(3):
                top = a * 32
                total[y + j + a] += (
                    shift(piece[top : top + 8], -1)
                    + piece[top + 8 : top + 16]
                    + shift(piece[top + 16 : top + 24], 1)
                )
        return carry

    part = rows // size // 2
    lax.fori_loop(0, part, regularize, 0)

    def second(q, carry):
        wait_all(send1, recv1, send1_sem, recv1_sem, q, False)
        data = take(recv1, q)
        value = dot(gram_h[...], data) + dot(gram_l[...], data)
        put(send2, recv2, q, value - lanes([known[q * group + c] for c in range(group)]))
        send_all(send2, recv2, send2_sem, recv2_sem, q)
        return carry

    lax.fori_loop(0, chunks, second, 0)

    lax.fori_loop(part, rows // size, regularize, 0)

    def unload(t, carry):
        y = pl.multiple_of(t * step16, step16)
        turned = jnp.swapaxes(total[pl.ds(y + 1, step16)], 0, 1)
        edges[1, :, pl.ds(y, step16)] = turned[0:2].astype(bf16)
        centre[:, pl.ds(y, step16)] = turned[2:4]
        edges[0, :, pl.ds(y, step16)] = turned[4:6].astype(bf16)
        return carry

    lax.fori_loop(0, rows // step16, unload, 0)
    for copy in edge_copies:
        copy.start()

    for copy in edge_copies:
        copy.wait()
    regular = (
        centre[...]
        + edges_in[0].astype(f32) * has_below
        + edges_in[1].astype(f32) * has_above
    )
    out[...] = estimate[...] - reg_weight * regular

    def third(q, carry):
        wait_all(send2, recv2, send2_sem, recv2_sem, q, False)
        data = take(recv2, q)
        errors = dot(line_ht[...], data) + dot(line_lt[...], data)
        real, imag = 0.0, 0.0
        for c in range(group):
            error = errors[:, c * columns : (c + 1) * columns]
            map_real, map_imag = maps[0, q * group + c], maps[1, q * group + c]
            real += map_real * error[:rows] + map_imag * error[rows:]
            imag += map_real * error[rows:] - map_imag * error[:rows]
        out[0] -= step_size * real
        out[1] -= step_size * imag
        return carry

    lax.fori_loop(0, chunks, third, 0)

    def drain(q, carry):
        wait_all(send1, recv1, send1_sem, recv1_sem, q, True)
        wait_all(send2, recv2, send2_sem, recv2_sem, q, True)
        return carry

    lax.fori_loop(0, chunks, drain, 0)


def fused(estimate, coil_maps, measured, sampled, plane_kernel, depth_kernel, depth_offset):
    devices = lax.axis_size("cuts")
    _, _, rows, columns = estimate.shape
    coils = coil_maps.shape[1]
    depth, lines = sampled.shape
    channels = plane_kernel.shape[3]
    chunks = 4
    table = line_table(rows, devices)
    mix = depth_table(depth, lines)
    mask = jnp.broadcast_to(sampled.astype(f32)[None], (2, depth, lines)).reshape(1, -1)
    wide = jnp.pad(plane_kernel, ((0, 0), (0, 1), (0, 0), (0, 0)))
    taps = np.eye(4, 3, dtype=np.float32)
    spread = (
        wide[:, :, None, :, None, :] * jnp.asarray(taps, bf16)[None, None, :, None, :, None]
    ).reshape(96, 3 * channels)
    depth_rows = depth_kernel.reshape(3 * channels, channels)
    read = readout_table(columns)
    squares = [table, table.T, mix.T, mix, read[:, :columns], read[:, columns:]]
    tables = np.stack([part for square in squares for part in halves(square)])
    rest = [
        mask,
        spread,
        spread.T,
        depth_rows,
        depth_offset[:, None],
    ]
    size = 2 * rows
    packet = (chunks, devices, coils // chunks * 2 * lines, columns)
    vmem = pltpu.VMEM
    pair = pltpu.SemaphoreType.DMA((chunks, devices))
    two = pltpu.SemaphoreType.DMA((2,))
    square = vmem((size, size), bf16)
    result = pl.pallas_call(
        functools.partial(kernel, chunks),
        out_shape=jax.ShapeDtypeStruct((2, rows, columns), f32),
        in_specs=[pl.BlockSpec(memory_space=pl.ANY)] * 4
        + [pl.BlockSpec(memory_space=vmem)] * len(rest),
        out_specs=pl.BlockSpec(memory_space=vmem),
        scratch_shapes=[
            vmem((2, rows, columns), f32),
            vmem(tables.shape, bf16),
            vmem((2, coils, rows, columns), f32),
            vmem(measured.shape, f32),
            vmem((coils, size, columns), f32),
            square,
            square,
            square,
            square,
            vmem(packet, bf16),
            vmem(packet, bf16),
            vmem(packet, bf16),
            vmem(packet, bf16),
            vmem((2, rows, columns), bf16),
            vmem((2, 2, rows, columns), bf16),
            vmem((rows + 2, 32, columns), bf16),
            vmem((rows + 2, 8, columns), f32),
            vmem((2, 2, rows, columns), bf16),
            vmem((2, 2, rows, columns), bf16),
            vmem((2, rows, columns), f32),
            pltpu.SemaphoreType.DMA((chunks,)),
            pltpu.SemaphoreType.DMA,
            pltpu.SemaphoreType.DMA,
            pltpu.SemaphoreType.DMA,
            pltpu.SemaphoreType.DMA,
            pair,
            pair,
            pair,
            pair,
            two,
            two,
            two,
            two,
        ],
        compiler_params=pltpu.CompilerParams(
            collective_id=0, has_side_effects=True, vmem_limit_bytes=52 * 2**20
        ),
    )(estimate[:, 0], coil_maps[:, :, 0], measured, jnp.asarray(tables), *rest)
    return result[:, None]


def shards(estimate, coil_maps, measured, sampled, plane_kernel, depth_kernel, depth_offset):
    devices = lax.axis_size("cuts")
    _, slices, rows, columns = estimate.shape
    coils = coil_maps.shape[1]
    depth, lines = sampled.shape
    if slices == 1 and 2 * lines % 16 == 0 and rows % 16 == 0 and coils % 4 == 0 and columns == 2 * rows:
        return fused(
            estimate, coil_maps, measured, sampled, plane_kernel, depth_kernel, depth_offset
        )
    table = line_table(rows, devices)
    maps_real, maps_imag = coil_maps[0], coil_maps[1]
    image_real, image_imag = estimate[0][None], estimate[1][None]
    coil = jnp.concatenate(
        [
            maps_real * image_real - maps_imag * image_imag,
            maps_real * image_imag + maps_imag * image_real,
        ],
        axis=2,
    )
    sent = product3("ky,czyx->kczx", table, coil).astype(bf16)
    sent = sent.reshape(devices, 2 * lines, coils, slices, columns).transpose(0, 3, 2, 1, 4)
    arrived = lax.all_to_all(sent, "cuts", split_axis=0, concat_axis=0, tiled=True)
    mix = depth_table(depth, lines)
    mask = jnp.broadcast_to(sampled.astype(f32)[None], (2, depth, lines)).reshape(-1, 1)
    masked = mix * mask
    gram = jnp.einsum("kr,kq->rq", mix, masked, precision=lax.Precision.HIGHEST)
    readout = product3(
        "kx,xn->kn", measured.reshape(2 * coils * depth * lines, columns), readout_table(columns)
    ).reshape(2, coils, depth, lines, 2, columns)
    cosines, sines = readout[:, :, :, :, 0], readout[:, :, :, :, 1]
    known = jnp.stack([cosines[0] - sines[1], cosines[1] + sines[0]])
    known = product3(
        "kr,kcx->rcx",
        masked,
        known.transpose(0, 2, 3, 1, 4).reshape(2 * depth * lines, coils, columns),
    )
    data = arrived.reshape(depth, coils, 2 * lines, columns).transpose(0, 2, 1, 3)
    data = data.reshape(2 * depth * lines, coils, columns)
    high, low = halves(gram)
    residual = product("rq,qcx->rcx", high, data) + product("rq,qcx->rcx", low, data) - known
    back = residual.astype(bf16).reshape(devices, slices, 2 * lines, coils, columns)
    back = lax.all_to_all(back, "cuts", split_axis=0, concat_axis=0, tiled=True)
    back = back.transpose(0, 2, 1, 3, 4).reshape(2 * rows, slices, coils, columns)
    high, low = halves(table)
    errors = product("ky,kzcx->yczx", high, back) + product("ky,kzcx->yczx", low, back)
    errors = errors.reshape(2, rows, coils, slices, columns).transpose(0, 2, 3, 1, 4)
    grad_real = jnp.sum(maps_real * errors[0] + maps_imag * errors[1], axis=0)
    grad_imag = jnp.sum(maps_real * errors[1] - maps_imag * errors[0], axis=0)
    gradient = jnp.stack([grad_real, grad_imag])
    regular = regular_term(estimate, plane_kernel, depth_kernel, depth_offset)
    return estimate - step_size * gradient - reg_weight * regular


def solution(mesh):
    return jax.shard_map(
        shards,
        mesh=mesh,
        in_specs=(
            P("groups", "cuts", None, None),
            P("groups", None, "cuts", None, None),
            P("groups", None, None, "cuts", None),
            P("groups", "cuts"),
            P(),
            P(),
            P(),
        ),
        out_specs=P("groups", "cuts", None, None),
        check_vma=False,
    )
```

```python
import functools
import math

import jax
import jax.numpy as jnp
import ml_dtypes
import numpy as np
from jax import lax
from jax.experimental import pallas as pl
from jax.experimental.pallas import tpu as pltpu
from jax.sharding import PartitionSpec as P

step_size = 0.5
reg_weight = 0.25
bf16 = jnp.bfloat16
f32 = jnp.float32


def halves(table):
    if isinstance(table, np.ndarray):
        high = table.astype(ml_dtypes.bfloat16)
        return high, (table - high.astype(np.float32)).astype(ml_dtypes.bfloat16)
    high = jnp.asarray(table, f32).astype(bf16)
    low = (jnp.asarray(table, f32) - high.astype(f32)).astype(bf16)
    return high, low


def real_form(angles, factor):
    cos, sin = np.cos(angles) * factor, np.sin(angles) * factor
    return np.stack([np.stack([cos, sin]), np.stack([-sin, cos])])


def fourier(length):
    index = np.arange(length)
    angles = (index[:, None] * index[None, :] % length) * (2.0 * math.pi / length)
    return real_form(angles, 1.0 / math.sqrt(length))


def line_table(length, devices):
    blocks = fourier(length).transpose(0, 2, 1, 3)
    lines = length // devices
    blocks = blocks.reshape(2, devices, lines, 2 * length).transpose(1, 0, 2, 3)
    return blocks.reshape(2 * length, 2 * length).astype(np.float32)


def depth_table(depth, lines):
    table = fourier(depth)
    whole = np.einsum("pqkz,lm->pklzqm", table, np.eye(lines))
    return whole.reshape(2 * depth * lines, 2 * depth * lines).astype(np.float32)


def readout_table(length):
    table = fourier(length)
    return np.concatenate([table[0, 0], table[0, 1]], axis=1).astype(np.float32)


def product(pattern, a, b):
    return jnp.einsum(pattern, a, b, preferred_element_type=f32)


def product3(pattern, a, b):
    ah, al = halves(a)
    bh, bl = halves(b)
    return product(pattern, ah, bh) + product(pattern, al, bh) + product(pattern, ah, bl)


def with_halo(x, axis, dim):
    devices, length = lax.axis_size(axis), x.shape[dim]
    up = [(i, i + 1) for i in range(devices - 1)]
    down = [(j, i) for i, j in up]
    last = lax.slice_in_dim(x, length - 1, length, axis=dim)
    initial = lax.slice_in_dim(x, 0, 1, axis=dim)
    before = lax.ppermute(last, axis, up)
    after = lax.ppermute(initial, axis, down)
    return jnp.concatenate([before, x, after], axis=dim)


def regular_term(estimate, plane_kernel, depth_kernel, depth_offset):
    _, slices, rows, columns = estimate.shape
    channels = plane_kernel.shape[3]
    image = with_halo(estimate.astype(bf16), "cuts", 1)
    padded = jnp.pad(image, ((0, 0), (0, 0), (1, 1), (1, 1)))
    shifted = jnp.concatenate(
        [padded[:, :, a : a + rows, b : b + columns] for a in range(3) for b in range(3)], axis=0
    )
    flat = plane_kernel.reshape(18, channels)
    features = product("kc,kzyx->czyx", flat, shifted).astype(bf16)
    taps = jnp.concatenate([features[:, k : k + slices] for k in range(3)], axis=0)
    preact = depth_offset[:, None, None, None] + product(
        "kc,kzyx->czyx", depth_kernel.reshape(3 * channels, channels), taps
    )
    activation = jnp.tanh(preact).astype(bf16)
    joint = jnp.einsum(
        "abim,kmc->abkic",
        plane_kernel.astype(f32),
        depth_kernel.astype(f32),
        precision=lax.Precision.HIGHEST,
    )
    high, low = halves(joint.reshape(54, channels))
    both = jnp.concatenate([high, low], axis=1)
    spread = product("rc,czyx->rzyx", both, jnp.concatenate([activation, activation], axis=0))
    spread = spread.reshape(3, 3, 3, 2, slices, rows, columns)
    spread = jnp.pad(spread, [(0, 0)] * 5 + [(1, 1), (1, 1)])
    total = sum(
        spread[a, b, :, :, :, 2 - a : 2 - a + rows, 2 - b : 2 - b + columns]
        for a in range(3)
        for b in range(3)
    )
    devices = lax.axis_size("cuts")
    up = [(i, i + 1) for i in range(devices - 1)]
    below = lax.ppermute(total[2][:, slices - 1 :], "cuts", up)
    above = lax.ppermute(total[0][:, :1], "cuts", [(j, i) for i, j in up])
    regular = total[1] + jnp.concatenate([below, total[2][:, : slices - 1]], axis=1)
    return regular + jnp.concatenate([total[0][:, 1:], above], axis=1)


def dot(a, b):
    return jnp.dot(a, b, preferred_element_type=f32)


def kernel(
    chunks,
    estimate_any,
    maps_any,
    measured_any,
    tables_any,
    mask,
    spread,
    spread_t,
    depth_rows,
    offset,
    out,
    estimate,
    tables,
    maps,
    measured,
    known,
    gram_h,
    mixed_h,
    mixed_l,
    send1,
    recv1,
    send2,
    recv2,
    image,
    halo,
    patches,
    total,
    edges,
    edges_in,
    centre,
    map_sem,
    measured_sem,
    estimate_sem,
    line_sem,
    table_sem,
    send1_sem,
    recv1_sem,
    send2_sem,
    recv2_sem,
    halo_send,
    halo_recv,
    edge_send,
    edge_recv,
):
    devices = send1.shape[1]
    me = lax.axis_index("cuts")
    above, below = lax.rem(me + 1, devices), lax.rem(me + devices - 1, devices)
    _, rows, columns = estimate.shape
    coils = maps.shape[1]
    bits = devices.bit_length() - 1

    def partner(step):
        if devices != 2**bits:
            return lax.rem(me + step, devices)
        device = 0
        for bit in range(bits):
            flip = (step // 2 ** (bits - 1 - bit)) % 2
            device += 2**bit * ((me // 2**bit + flip) % 2)
        return device

    group = coils // chunks
    block = send1.shape[2] // group

    def map_copy(q):
        part = pl.ds(q * group, group)
        return pltpu.make_async_copy(maps_any.at[:, part], maps.at[:, part], map_sem.at[q])

    def table_copy(first, count, sem):
        part = pl.ds(first, count)
        return pltpu.make_async_copy(tables_any.at[part], tables.at[part], sem)

    measured_copy = pltpu.make_async_copy(measured_any, measured, measured_sem)
    estimate_copy = pltpu.make_async_copy(estimate_any, estimate, estimate_sem)
    line_copy = table_copy(0, 2, line_sem)
    rest_copy = table_copy(2, tables.shape[0] - 2, table_sem)
    line_h, line_l, line_ht, line_lt = (tables.at[i] for i in range(4))
    mix_ht, mix_lt, mix_h, mix_l = (tables.at[i] for i in range(4, 8))
    estimate_copy.start()
    line_copy.start()
    for q in range(chunks):
        map_copy(q).start()
    rest_copy.start()
    measured_copy.start()

    barrier = pltpu.get_barrier_semaphore()

    def greet(step, carry):
        pl.semaphore_signal(
            barrier,
            inc=1,
            device_id={"cuts": lax.rem(me + step, devices)},
            device_id_type=pl.DeviceIdType.MESH,
        )
        return carry

    lax.fori_loop(1, devices, greet, 0)
    estimate_copy.wait()
    image[...] = estimate[...].astype(bf16)
    line_copy.wait()

    def remote(source, target, send_sem, recv_sem, device):
        return pltpu.make_async_remote_copy(
            src_ref=source,
            dst_ref=target,
            send_sem=send_sem,
            recv_sem=recv_sem,
            device_id={"cuts": device},
            device_id_type=pl.DeviceIdType.MESH,
        )

    halo_copies = [
        remote(image, halo.at[0], halo_send.at[0], halo_recv.at[0], above),
        remote(image, halo.at[1], halo_send.at[1], halo_recv.at[1], below),
    ]
    edge_copies = [
        remote(edges.at[0], edges_in.at[0], edge_send.at[0], edge_recv.at[0], above),
        remote(edges.at[1], edges_in.at[1], edge_send.at[1], edge_recv.at[1], below),
    ]

    def send_all(source, target, send_sem, recv_sem, q):
        def body(step, carry):
            device = partner(step)
            remote(
                source.at[q, device],
                target.at[q, me],
                send_sem.at[q, device],
                recv_sem.at[q, me],
                device,
            ).start()
            return carry

        lax.fori_loop(1, devices, body, 0)

    def wait_all(source, target, send_sem, recv_sem, q, sent):
        def body(step, carry):
            device = lax.rem(me + step, devices)
            copy = remote(
                source.at[q, device],
                target.at[q, device],
                send_sem.at[q, device],
                recv_sem.at[q, device],
                device,
            )
            if sent:
                copy.wait_send()
            else:
                copy.wait_recv()
            return carry

        lax.fori_loop(1, devices, body, 0)

    def lanes(pieces):
        return jnp.concatenate(pieces, axis=1)

    def put(target, mine, q, value):
        value = value.astype(bf16)
        for c in range(group):
            piece = value[:, c * columns : (c + 1) * columns]
            target[q, :, c * block : (c + 1) * block, :] = piece.reshape(devices, block, columns)
        mine[q, me] = target[q, me]

    def take(source, q):
        return lanes(
            [
                source[q, :, c * block : (c + 1) * block, :].reshape(devices * block, columns)
                for c in range(group)
            ]
        )

    def first(q):
        map_copy(q).wait()
        pieces = []
        for c in range(group):
            real, imag = maps[0, q * group + c], maps[1, q * group + c]
            pieces.append(
                jnp.concatenate(
                    [
                        real * estimate[0] - imag * estimate[1],
                        real * estimate[1] + imag * estimate[0],
                    ],
                    axis=0,
                )
            )
        put(send1, recv1, q, dot(line_h[...], lanes(pieces).astype(bf16)))

    first(0)
    pl.semaphore_wait(barrier, devices - 1)
    send_all(send1, recv1, send1_sem, recv1_sem, 0)
    for copy in halo_copies:
        copy.start()

    def first_rest(q, carry):
        first(q)
        send_all(send1, recv1, send1_sem, recv1_sem, q)
        return carry

    lax.fori_loop(1, chunks, first_rest, 0)

    rest_copy.wait()
    masked_h = mix_ht[...].astype(f32) * mask[...]
    masked_l = mix_lt[...].astype(f32) * mask[...]
    mixed_h[...] = masked_h.astype(bf16)
    mixed_l[...] = masked_l.astype(bf16)
    gram_h[...] = (
        dot(mixed_h[...], mix_h[...]) + dot(mixed_l[...], mix_h[...]) + dot(mixed_h[...], mix_l[...])
    ).astype(bf16)
    measured_copy.wait()

    def acquire(q, carry):
        size = devices * block
        value = jnp.concatenate(
            [measured[:, q * group + c].reshape(size, columns) for c in range(group)], axis=0
        ).astype(bf16)
        cos, sin = dot(value, tables[8]), dot(value, tables[10])
        half = size // 2
        turned = []
        for c in range(group):
            top, middle, end = c * size, c * size + half, (c + 1) * size
            turned.append(
                jnp.concatenate(
                    [cos[top:middle] - sin[middle:end], cos[middle:end] + sin[top:middle]], axis=0
                ).astype(bf16)
            )
        kept = dot(mixed_h[...], lanes(turned))
        for c in range(group):
            known[q * group + c] = kept[:, c * columns : (c + 1) * columns]
        return carry

    lax.fori_loop(0, chunks, acquire, 0)

    for copy in halo_copies:
        copy.wait()
    has_below = jnp.where(me > 0, 1.0, 0.0).astype(f32)
    has_above = jnp.where(me < devices - 1, 1.0, 0.0).astype(f32)
    patches[0] = jnp.zeros(patches.shape[1:], bf16)
    patches[rows + 1] = jnp.zeros(patches.shape[1:], bf16)
    total[...] = jnp.zeros_like(total)
    step16 = 16

    def shift(value, way):
        axis = value.ndim - 1
        lane = lax.broadcasted_iota(jnp.int32, value.shape, axis)
        if way > 0:
            return jnp.where(lane == 0, 0.0, pltpu.roll(value, 1, axis))
        return jnp.where(lane == columns - 1, 0.0, pltpu.roll(value, columns - 1, axis))

    def build(t, carry):
        y = pl.multiple_of(t * step16, step16)
        stacked = jnp.concatenate(
            [
                halo[0, :, pl.ds(y, step16)].astype(f32) * has_below,
                image[:, pl.ds(y, step16)].astype(f32),
                halo[1, :, pl.ds(y, step16)].astype(f32) * has_above,
                jnp.zeros((2, step16, columns), f32),
            ],
            axis=0,
        )
        turned = jnp.swapaxes(stacked, 0, 1)
        left = shift(turned.reshape(step16 * 8, columns), 1).reshape(turned.shape)
        right = shift(turned.reshape(step16 * 8, columns), -1).reshape(turned.shape)
        patches[pl.ds(y + 1, step16)] = jnp.concatenate(
            [left, turned, right, jnp.zeros_like(turned)], axis=1
        ).astype(bf16)
        return carry

    lax.fori_loop(0, rows // step16, build, 0)
    joint = dot(spread[...], depth_rows[...]).astype(bf16)
    size = 8

    def regularize(t, carry):
        y = t * size
        patch = lanes(
            [
                jnp.concatenate([patches[y + j + a] for a in range(3)], axis=0)
                for j in range(size)
            ]
        )
        features = dot(spread_t[...], patch).astype(bf16)
        activation = jnp.tanh(lax.dot_general(depth_rows[...], features, (((0,), (0,)), ((), ())), preferred_element_type=f32) + offset[...]).astype(bf16)
        back = dot(joint, activation)
        for row in range(size + 2):
            value = sum(
                back[a * 32 : a * 32 + 24, (row - a) * columns : (row - a + 1) * columns]
                for a in range(3)
                if 0 <= row - a < size
            )
            value = shift(value[:8], -1) + value[8:16] + shift(value[16:], 1)
            if row < 2:
                value += total[y + row]
            total[y + row] = value
        return carry

    part = rows // size // 2
    lax.fori_loop(0, part, regularize, 0)

    def second(q, carry):
        wait_all(send1, recv1, send1_sem, recv1_sem, q, False)
        data = take(recv1, q)
        value = dot(gram_h[...], data)
        put(send2, recv2, q, value - lanes([known[q * group + c] for c in range(group)]))
        send_all(send2, recv2, send2_sem, recv2_sem, q)
        return carry

    lax.fori_loop(0, chunks, second, 0)

    lax.fori_loop(part, rows // size, regularize, 0)

    def unload(t, carry):
        y = pl.multiple_of(t * step16, step16)
        turned = jnp.swapaxes(total[pl.ds(y + 1, step16)], 0, 1)
        edges[1, :, pl.ds(y, step16)] = turned[0:2].astype(bf16)
        centre[:, pl.ds(y, step16)] = turned[2:4]
        edges[0, :, pl.ds(y, step16)] = turned[4:6].astype(bf16)
        return carry

    lax.fori_loop(0, rows // step16, unload, 0)
    for copy in edge_copies:
        copy.start()

    for copy in edge_copies:
        copy.wait()
    regular = (
        centre[...]
        + edges_in[0].astype(f32) * has_below
        + edges_in[1].astype(f32) * has_above
    )
    out[...] = estimate[...] - reg_weight * regular

    def third(q, carry):
        wait_all(send2, recv2, send2_sem, recv2_sem, q, False)
        data = take(recv2, q)
        errors = dot(line_ht[...], data) + dot(line_lt[...], data)
        real, imag = 0.0, 0.0
        for c in range(group):
            error = errors[:, c * columns : (c + 1) * columns]
            map_real, map_imag = maps[0, q * group + c], maps[1, q * group + c]
            real += map_real * error[:rows] + map_imag * error[rows:]
            imag += map_real * error[rows:] - map_imag * error[:rows]
        out[0] -= step_size * real
        out[1] -= step_size * imag
        return carry

    lax.fori_loop(0, chunks, third, 0)

    def drain(q, carry):
        wait_all(send1, recv1, send1_sem, recv1_sem, q, True)
        wait_all(send2, recv2, send2_sem, recv2_sem, q, True)
        return carry

    lax.fori_loop(0, chunks, drain, 0)


def fused(estimate, coil_maps, measured, sampled, plane_kernel, depth_kernel, depth_offset):
    devices = lax.axis_size("cuts")
    _, _, rows, columns = estimate.shape
    coils = coil_maps.shape[1]
    depth, lines = sampled.shape
    channels = plane_kernel.shape[3]
    chunks = 4
    table = line_table(rows, devices)
    mix = depth_table(depth, lines)
    mask = jnp.broadcast_to(sampled.astype(f32)[None], (2, depth, lines)).reshape(1, -1)
    wide = jnp.pad(plane_kernel, ((0, 0), (0, 1), (0, 0), (0, 0)))
    taps = np.eye(4, 3, dtype=np.float32)
    spread = (
        wide[:, :, None, :, None, :] * jnp.asarray(taps, bf16)[None, None, :, None, :, None]
    ).reshape(96, 3 * channels)
    depth_rows = depth_kernel.reshape(3 * channels, channels)
    read = readout_table(columns)
    squares = [table, table.T, mix.T, mix, read[:, :columns], read[:, columns:]]
    tables = np.stack([part for square in squares for part in halves(square)])
    rest = [
        mask,
        spread,
        spread.T,
        depth_rows,
        depth_offset[:, None],
    ]
    size = 2 * rows
    packet = (chunks, devices, coils // chunks * 2 * lines, columns)
    vmem = pltpu.VMEM
    pair = pltpu.SemaphoreType.DMA((chunks, devices))
    two = pltpu.SemaphoreType.DMA((2,))
    square = vmem((size, size), bf16)
    result = pl.pallas_call(
        functools.partial(kernel, chunks),
        out_shape=jax.ShapeDtypeStruct((2, rows, columns), f32),
        in_specs=[pl.BlockSpec(memory_space=pl.ANY)] * 4
        + [pl.BlockSpec(memory_space=vmem)] * len(rest),
        out_specs=pl.BlockSpec(memory_space=vmem),
        scratch_shapes=[
            vmem((2, rows, columns), f32),
            vmem(tables.shape, bf16),
            vmem((2, coils, rows, columns), f32),
            vmem(measured.shape, f32),
            vmem((coils, size, columns), f32),
            square,
            square,
            square,
            vmem(packet, bf16),
            vmem(packet, bf16),
            vmem(packet, bf16),
            vmem(packet, bf16),
            vmem((2, rows, columns), bf16),
            vmem((2, 2, rows, columns), bf16),
            vmem((rows + 2, 32, columns), bf16),
            vmem((rows + 2, 8, columns), f32),
            vmem((2, 2, rows, columns), bf16),
            vmem((2, 2, rows, columns), bf16),
            vmem((2, rows, columns), f32),
            pltpu.SemaphoreType.DMA((chunks,)),
            pltpu.SemaphoreType.DMA,
            pltpu.SemaphoreType.DMA,
            pltpu.SemaphoreType.DMA,
            pltpu.SemaphoreType.DMA,
            pair,
            pair,
            pair,
            pair,
            two,
            two,
            two,
            two,
        ],
        compiler_params=pltpu.CompilerParams(
            collective_id=0, has_side_effects=True, vmem_limit_bytes=52 * 2**20
        ),
    )(estimate[:, 0], coil_maps[:, :, 0], measured, jnp.asarray(tables), *rest)
    return result[:, None]


def shards(estimate, coil_maps, measured, sampled, plane_kernel, depth_kernel, depth_offset):
    devices = lax.axis_size("cuts")
    _, slices, rows, columns = estimate.shape
    coils = coil_maps.shape[1]
    depth, lines = sampled.shape
    if slices == 1 and 2 * lines % 16 == 0 and rows % 16 == 0 and coils % 4 == 0 and columns == 2 * rows:
        return fused(
            estimate, coil_maps, measured, sampled, plane_kernel, depth_kernel, depth_offset
        )
    table = line_table(rows, devices)
    maps_real, maps_imag = coil_maps[0], coil_maps[1]
    image_real, image_imag = estimate[0][None], estimate[1][None]
    coil = jnp.concatenate(
        [
            maps_real * image_real - maps_imag * image_imag,
            maps_real * image_imag + maps_imag * image_real,
        ],
        axis=2,
    )
    sent = product3("ky,czyx->kczx", table, coil).astype(bf16)
    sent = sent.reshape(devices, 2 * lines, coils, slices, columns).transpose(0, 3, 2, 1, 4)
    arrived = lax.all_to_all(sent, "cuts", split_axis=0, concat_axis=0, tiled=True)
    mix = depth_table(depth, lines)
    mask = jnp.broadcast_to(sampled.astype(f32)[None], (2, depth, lines)).reshape(-1, 1)
    masked = mix * mask
    gram = jnp.einsum("kr,kq->rq", mix, masked, precision=lax.Precision.HIGHEST)
    readout = product3(
        "kx,xn->kn", measured.reshape(2 * coils * depth * lines, columns), readout_table(columns)
    ).reshape(2, coils, depth, lines, 2, columns)
    cosines, sines = readout[:, :, :, :, 0], readout[:, :, :, :, 1]
    known = jnp.stack([cosines[0] - sines[1], cosines[1] + sines[0]])
    known = product3(
        "kr,kcx->rcx",
        masked,
        known.transpose(0, 2, 3, 1, 4).reshape(2 * depth * lines, coils, columns),
    )
    data = arrived.reshape(depth, coils, 2 * lines, columns).transpose(0, 2, 1, 3)
    data = data.reshape(2 * depth * lines, coils, columns)
    high, low = halves(gram)
    residual = product("rq,qcx->rcx", high, data) + product("rq,qcx->rcx", low, data) - known
    back = residual.astype(bf16).reshape(devices, slices, 2 * lines, coils, columns)
    back = lax.all_to_all(back, "cuts", split_axis=0, concat_axis=0, tiled=True)
    back = back.transpose(0, 2, 1, 3, 4).reshape(2 * rows, slices, coils, columns)
    high, low = halves(table)
    errors = product("ky,kzcx->yczx", high, back) + product("ky,kzcx->yczx", low, back)
    errors = errors.reshape(2, rows, coils, slices, columns).transpose(0, 2, 3, 1, 4)
    grad_real = jnp.sum(maps_real * errors[0] + maps_imag * errors[1], axis=0)
    grad_imag = jnp.sum(maps_real * errors[1] - maps_imag * errors[0], axis=0)
    gradient = jnp.stack([grad_real, grad_imag])
    regular = regular_term(estimate, plane_kernel, depth_kernel, depth_offset)
    return estimate - step_size * gradient - reg_weight * regular


def solution(mesh):
    return jax.shard_map(
        shards,
        mesh=mesh,
        in_specs=(
            P("groups", "cuts", None, None),
            P("groups", None, "cuts", None, None),
            P("groups", None, None, "cuts", None),
            P("groups", "cuts"),
            P(),
            P(),
            P(),
        ),
        out_specs=P("groups", "cuts", None, None),
        check_vma=False,
    )
```
